1024 devices in a mesh: dp: 8 (over y), expert: 32 (over z, core), tensor: 4 (over x).
Axes of the slice: x: 4, y: 8, z: 16, core: 2. Of those that a mesh axis runs over, the one named last changes fastest.
Arguments:
- out_grad: bfloat16 [32768, 3584], P(('dp', 'expert'), 'tensor'), may hold values from -6 to 6
- route_ids: int32 [32768, 2], P(('dp', 'expert')), may hold values from 0 to 31, all different within a row; in each aligned block of 128 rows (0 to 127, 128 to 255, ...) at most 12 rows name the same one
- route_probs: float32 [32768, 2], P(('dp', 'expert')), may hold values from 0.2 to 1
- dense_gate_pre: bfloat16 [32768, 2432], P(('dp', 'expert'), 'tensor'), may hold values from -6 to 6
- dense_up_pre: bfloat16 [32768, 2432], P(('dp', 'expert'), 'tensor'), may hold values from -6 to 6
- dense_down: bfloat16 [2432, 3584], P('tensor', ('dp', 'expert')), may hold values from -0.09375 to 0.09375
- expert_gate_pre: bfloat16 [8, 32, 384, 2432], P('dp', 'expert', None, 'tensor'), may hold values from -6 to 6
- expert_up_pre: bfloat16 [8, 32, 384, 2432], P('dp', 'expert', None, 'tensor'), may hold values from -6 to 6
- expert_down: bfloat16 [32, 2432, 3584], P('expert', 'tensor'), may hold values from -0.09375 to 0.09375
Outputs:
- dense_gate_grad: bfloat16 [32768, 2432], P(('dp', 'expert'), 'tensor')
- dense_up_grad: bfloat16 [32768, 2432], P(('dp', 'expert'), 'tensor')
- expert_gate_grad: bfloat16 [8, 32, 384, 2432], P('dp', 'expert', None, 'tensor')
- expert_up_grad: bfloat16 [8, 32, 384, 2432], P('dp', 'expert', None, 'tensor')
The draws below stay inside these ranges and needn't reach their ends.
Inputs may be any that keep to these rules, and one draw needn't show every extreme that they name: `route_ids`: each row names 2 different experts. In the rows of one device no expert is named more than 12 times, a bound that some block reaches.
All inputs are finite; a program needn't handle non-finite values.
Results may differ from the reference program's by a relative error of at most 0.0049.
Values may be sent and summed in bfloat16 or wider, within the bound.
A program may use at most 64 MiB of HBM per device.

```python
import math
import jax
import jax.numpy as jnp
import numpy as np
from jax import lax

DW = 3584
FE = 2432
FR = 2432
TOP = 2
TOK_DEV = 128
EXPERTS = 32
CAP = 12
SLOTS = 384
TOKENS = 32768
N_DP = 8
N_EXPERT = 32


def levels(own_key, shape, shards, least, top_value):
    factor_of = 1.0
    for dim, parts in shards:
        heights = jax.random.uniform(jax.random.fold_in(jax.random.fold_in(own_key, 6), dim), (parts,), jnp.float32, least / len(shards), top_value / len(shards))
        factor_of = factor_of * jnp.repeat(jnp.exp(heights), shape[dim] // parts).reshape((-1,) + (1,) * (len(shape) - 1 - dim))
    return factor_of


def deal_out(key, own, number, rows, amount, top, limit, lean):
    order = jax.random.permutation(key, amount)
    packed, common = load_shares(amount, rows * top, limit, lean, True), load_shares(amount, rows * top, limit, lean, False)
    places = jnp.arange(amount)

    def named(sizes, offset_by):
        used = int((sizes > 0).sum())
        fixed = max(1, used // 4)
        shifted = fixed + (places - fixed + offset_by * (used - fixed)) % max(1, amount - fixed)
        return jnp.zeros((amount,), jnp.int32).at[order[jnp.where(places < fixed, places, shifted)]].set(jnp.asarray(sizes, jnp.int32))

    sizes = jnp.where(number % 4 == 0, named(packed, number // 4), named(common, number - number // 4 - 1))
    mixed = jax.random.permutation(jax.random.fold_in(own, 3), amount)
    giver, sink = mixed[0:amount // 2 * 2:2], mixed[1:amount // 2 * 2:2]
    margin = jnp.minimum(sizes[giver] - 1, limit - sizes[sink]) // 2
    margin = jnp.where((giver == order[0]) | (sink == order[0]) | (sizes[sink] == 0), 0, jnp.maximum(margin, 0))
    shifted = jax.random.randint(jax.random.fold_in(own, 4), (amount // 2,), 0, 1 << 20) % (margin + 1)
    sizes = sizes.at[giver].add(-shifted).at[sink].add(shifted)
    items = jnp.searchsorted(jnp.cumsum(sizes), jnp.arange(rows * top), side="right").astype(jnp.int32)
    table = items.reshape(top, rows).T
    table = table[jax.random.permutation(jax.random.fold_in(own, 1), rows)]
    offset_by = jax.random.randint(jax.random.fold_in(own, 2), (rows, 1), 0, top)
    return jnp.take_along_axis(table, (jnp.arange(top)[None, :] + offset_by) % top, axis=1)


def load_shares(count, total, most, skew, full):
    weights = [(1 << 20) // math.isqrt(standing ** skew) + 1 for standing in range(1, count + 1)]
    largest = most if full else min(most, max(-(-total // count), total * weights[0] // sum(weights)))
    least = 1 if total - largest >= count - 1 else 0
    holding, surplus = [largest] + [least] * (count - 1), total - largest - least * (count - 1)
    while surplus > 0:
        candidates = [i for i in range(1, count) if holding[i] < largest] or [i for i in range(1, count) if holding[i] < most]
        whole, budget = sum([weights[i] for i in candidates]), surplus
        for i in candidates:
            addition = min(most - holding[i], max(1, budget * weights[i] // whole), surplus)
            holding[i] = holding[i] + addition
            surplus = surplus - addition
    return np.array(holding)


def normal_values(own_key, extent, scale, bound, split=(), kind=jnp.bfloat16):
    drawn = scale * jax.random.normal(own_key, extent, jnp.float32)
    if split:
        drawn = drawn * levels(own_key, extent, split, -0.22, 0.18)
    return jnp.clip(drawn, -bound, bound).astype(kind)


def setup_inputs(seed: int = 0) -> dict:
    arg_keys = jax.random.split(jax.random.key(seed), 10)
    out_grad = normal_values(arg_keys[0], (TOKENS, DW), 1.0, 6.0, ((0, 256), (1, 4)))
    route_ids_keys = jax.random.split(jax.random.fold_in(arg_keys[1], 1), TOKENS // TOK_DEV)
    route_ids_turns = jax.random.permutation(jax.random.fold_in(arg_keys[1], 3), TOKENS // TOK_DEV)
    route_ids = jax.vmap(lambda own, number: deal_out(jax.random.fold_in(arg_keys[1], 2), own, number, TOK_DEV, EXPERTS, TOP, CAP, 2))(route_ids_keys, route_ids_turns).reshape((TOKENS, TOP))
    route_probs = jnp.clip(0.2 + 0.8 * jax.random.uniform(arg_keys[2], (TOKENS, TOP), jnp.float32) ** levels(arg_keys[2], (TOKENS, TOP), ((0, 256),), -0.2, 0.2), 0.2, 1.0)
    dense_gate_pre = normal_values(arg_keys[3], (TOKENS, FR), 1.0, 6.0, ((0, 256), (1, 4)))
    dense_up_pre = normal_values(arg_keys[4], (TOKENS, FR), 1.0, 6.0, ((0, 256), (1, 4)))
    dense_down = normal_values(arg_keys[5], (FR, DW), DW ** -0.5, 0.09375, ((0, 4), (1, 256)))
    expert_gate_pre = normal_values(arg_keys[6], (N_DP, EXPERTS, SLOTS, FE), 1.0, 6.0, ((0, 8), (1, 32), (3, 4)))
    expert_up_pre = normal_values(arg_keys[7], (N_DP, EXPERTS, SLOTS, FE), 1.0, 6.0, ((0, 8), (1, 32), (3, 4)))
    expert_down = normal_values(arg_keys[8], (EXPERTS, FE, DW), DW ** -0.5, 0.09375, ((0, 32), (1, 4)))
    return dict(out_grad=out_grad, route_ids=route_ids, route_probs=route_probs, dense_gate_pre=dense_gate_pre, dense_up_pre=dense_up_pre, dense_down=dense_down, expert_gate_pre=expert_gate_pre, expert_up_pre=expert_up_pre, expert_down=expert_down)


def slot_table(route_ids, route_probs, experts, capacity, first_slot, slot_count):
    width = route_ids.shape[1]
    flat_ids = route_ids.reshape(-1)
    flat_probs = route_probs.reshape(-1).astype(jnp.float32)
    total_rows = flat_ids.shape[0]
    onehot = (flat_ids[:, None] == jnp.arange(experts, dtype=jnp.int32)[None, :]).astype(jnp.int32)
    earlier = jnp.cumsum(onehot, axis=0) - onehot
    position = jnp.sum(earlier * onehot, axis=1)
    slot_cell = flat_ids * capacity + position
    targets = (jnp.arange(experts, dtype=jnp.int32)[:, None] * capacity + first_slot
               + jnp.arange(slot_count, dtype=jnp.int32)[None, :]).reshape(-1)
    matches = targets[:, None] == slot_cell[None, :]
    token_of = (jnp.arange(total_rows, dtype=jnp.int32) // width).astype(jnp.int32)
    row_scale = jnp.sum(jnp.where(matches, flat_probs[None, :], jnp.float32(0.0)), axis=1)
    owner_row = jnp.sum(jnp.where(matches, token_of[None, :], 0), axis=1).astype(jnp.int32)
    return owner_row, row_scale


def swiglu_back(gate_pre, up_pre, hidden):
    gate_val = gate_pre.astype(jnp.float32)
    up_val = up_pre.astype(jnp.float32)
    sigma = jax.nn.sigmoid(gate_val)
    up_grad = hidden * gate_val * sigma
    gate_grad = hidden * up_val * sigma * (1.0 + gate_val * (1.0 - sigma))
    return gate_grad.astype(jnp.bfloat16), up_grad.astype(jnp.bfloat16)


def reference(out_grad, route_ids, route_probs, dense_gate_pre, dense_up_pre, dense_down,
              expert_gate_pre, expert_up_pre, expert_down):
    dense_hidden = jnp.dot(out_grad, dense_down.T, preferred_element_type=jnp.float32)
    dense_gate_grad, dense_up_grad = swiglu_back(dense_gate_pre, dense_up_pre, dense_hidden)

    groups = out_grad.reshape(N_DP, N_EXPERT, TOK_DEV, DW)
    group_ids = route_ids.reshape(N_DP, N_EXPERT, TOK_DEV, TOP)
    group_probs = route_probs.reshape(N_DP, N_EXPERT, TOK_DEV, TOP)

    def per_source(source_grad, source_ids, source_probs):
        owner_row, row_scale = slot_table(source_ids, source_probs, EXPERTS, CAP, 0, CAP)
        sent_rows = jnp.take(source_grad, owner_row, axis=0).astype(jnp.float32) * row_scale[:, None]
        return sent_rows.astype(jnp.bfloat16).reshape(EXPERTS, CAP, DW)

    def per_expert(operands):
        received, weight, gate_pre, up_pre = operands
        hidden = jnp.dot(received, weight.T, preferred_element_type=jnp.float32)
        return swiglu_back(gate_pre, up_pre, hidden)

    def per_group(operands):
        grads, ids, probs, gate_pre, up_pre = operands
        buffers = jax.vmap(per_source)(grads, ids, probs)
        received = jnp.transpose(buffers, (1, 0, 2, 3)).reshape(EXPERTS, N_EXPERT * CAP, DW)
        return lax.map(per_expert, (received, expert_down, gate_pre, up_pre))

    expert_gate_grad, expert_up_grad = lax.map(
        per_group, (groups, group_ids, group_probs, expert_gate_pre, expert_up_pre))
    return dense_gate_grad, dense_up_grad, expert_gate_grad, expert_up_grad
```

```python
import functools

import jax
import jax.numpy as jnp
from jax import lax
from jax.experimental import pallas as pl
from jax.experimental.pallas import tpu as pltpu
from jax.sharding import PartitionSpec as P

MESH = pl.DeviceIdType.MESH
F32 = jnp.float32
BF16 = jnp.bfloat16

Z_GROUPS = ((0, 3), (3, 7), (7, 11), (11, 16))
Z_READY = (1, 3, 5, 8)


def slot_of(offset):
    if offset == 0:
        return 0
    return 2 * offset - 1 if offset > 0 else -2 * offset


def iota(shape, dim):
    return lax.broadcasted_iota(jnp.int32, shape, dim)


def one_hot(mask):
    return jnp.where(mask, 1.0, 0.0).astype(BF16)


def nn(a, b):
    return jnp.dot(a, b, preferred_element_type=F32)


def nt(a, b):
    return lax.dot_general(a, b, (((1,), (1,)), ((), ())), preferred_element_type=F32)


def factors(gate_pre, up_pre):
    a = gate_pre.astype(F32)
    b = up_pre.astype(F32)
    sigma = 1.0 / (1.0 + jnp.exp(-a))
    return b * sigma * (1.0 + a * (1.0 - sigma)), a * sigma


def kernel(
    grad_in, ids_in, probs_in, dgate_in, dup_in, ddown_in, egate_in, eup_in, edown_in,
    dgate_out, dup_out, egate_out, eup_out,
    ids, probs, table, xs, sends, lands, rows, weight, acc, e_gate, e_up, fac_gate, fac_up,
    d_raw, d_gate, d_up, d_weight, g_buf, select, part, part_in,
    in_sem, sib_send, sib_recv, z_send, z_recv, y_send, y_recv, g_send, g_recv,
    x_send, x_recv, a_send, a_recv, p_send, p_recv,
):
    y = lax.axis_index("dp")
    e = lax.axis_index("expert")
    x = lax.axis_index("tensor")
    z, c = e // 2, e % 2
    sib = (y, e + 1 - 2 * c, x)
    z_dev = lambda zz: (y, 2 * zz + c, x)
    y_dev = lambda k: ((y + k + 8) % 8, e, x)
    x_dev = lambda k: (y, e, (x + k + 4) % 4)
    m_me, h_me, p_me = (z // 2) % 4, z // 8, z % 2

    def remote(src, dst, send, recv, dev):
        return pltpu.make_async_remote_copy(
            src_ref=src, dst_ref=dst, send_sem=send, recv_sem=recv, device_id=dev, device_id_type=MESH
        )

    def landed(ref, sem):
        pltpu.make_async_copy(ref, ref, sem).wait()

    barrier = pltpu.get_barrier_semaphore()

    def greet(k, carry):
        pl.semaphore_signal(barrier, inc=1, device_id=z_dev((z + k) % 16), device_id_type=MESH)
        return carry

    for dev in (sib, y_dev(1), y_dev(-1), x_dev(1), x_dev(-1)):
        pl.semaphore_signal(barrier, inc=1, device_id=dev, device_id_type=MESH)
    lax.fori_loop(1, 16, greet, 0)

    loads = [
        (ids_in, ids), (probs_in, probs), (grad_in, xs.at[c]), (ddown_in, d_raw),
        (egate_in, e_gate), (eup_in, e_up), (dgate_in, d_gate), (dup_in, d_up),
    ] + [(edown_in.at[:, pl.ds(896 * k, 896)], weight.at[k]) for k in range(4)]
    loads = [pltpu.make_async_copy(s, d, in_sem.at[i]) for i, (s, d) in enumerate(loads)]
    for copy in loads:
        copy.start()

    loads[3].wait()
    d_weight[y, 0] = jnp.concatenate(
        [
            jnp.concatenate([d_raw[...].astype(F32), jnp.zeros((14, 32), F32)], axis=1),
            jnp.zeros((2, 640), F32),
        ],
        axis=0,
    ).astype(BF16)

    loads[0].wait()
    loads[1].wait()
    experts = iota((32, 128), 0)
    first, second = experts == ids[0:1, :], experts == ids[1:2, :]
    named = one_hot(first) + one_hot(second)
    earlier = nn(named, one_hot(iota((128, 128), 0) < iota((128, 128), 1)))
    cell_of = lambda j, hot: ids[j : j + 1, :].astype(F32) * 12.0 + jnp.sum(
        jnp.where(hot, earlier, 0.0), axis=0, keepdims=True
    )
    table[c] = jnp.concatenate(
        [cell_of(0, first), cell_of(1, second), probs[...], jnp.zeros((4, 128), F32)], axis=0
    )
    loads[2].wait()

    pl.semaphore_wait(barrier, 20)

    swap = [
        remote(table.at[c], table.at[c], sib_send.at[0], sib_recv.at[0], sib),
        remote(xs.at[c], xs.at[c], sib_send.at[1], sib_recv.at[1], sib),
    ]
    for copy in swap:
        copy.start()

    def z_step(s):
        plus = remote(
            d_weight.at[y, slot_of(1 - s)], d_weight.at[y, 15 if s == 8 else slot_of(-s)],
            z_send, z_recv.at[2 * s - 2], z_dev((z + 1) % 16),
        )
        plus.start()
        if s < 8:
            remote(
                d_weight.at[y, slot_of(s - 1)], d_weight.at[y, slot_of(s)],
                z_send, z_recv.at[2 * s - 1], z_dev((z + 15) % 16),
            ).start()

    def z_wait(s):
        landed(d_weight.at[y, 0], z_recv.at[2 * s - 2])
        if s < 8:
            landed(d_weight.at[y, 0], z_recv.at[2 * s - 1])

    z_step(1)

    q = iota((1, 512), 1)
    slot = (q >> 4) & 15
    half_off = (slot + 1) >> 1
    zq = (z + jnp.where((slot & 1) == 1, half_off, 16 - half_off)) & 15
    target = jnp.where((q & 15) < 14, (((q >> 8) * 16 + zq) * 2 + c) * 14 + (q & 15), -1)
    for k in range(7):
        select[pl.ds(128 * k, 128), :] = one_hot(iota((128, 512), 0) + 128 * k == target)

    for copy in swap:
        copy.wait_recv()

    w = iota((256, 1), 0)
    place = w & 15
    base = (2 * (w >> 4) + c) * 12
    target_a = jnp.where(place < 12, base + place, base + place - 12).astype(F32)
    target_b = (base + 4 + (place & 7)).astype(F32)

    def matched(core, wanted):
        tab = table[core]
        hit0, hit1 = tab[0:1, :] == wanted, tab[1:2, :] == wanted
        scale = jnp.sum(
            jnp.where(hit0, tab[2:3, :], 0.0) + jnp.where(hit1, tab[3:4, :], 0.0), axis=1, keepdims=True
        )
        return one_hot(hit0 | hit1), scale

    hot0, scale0 = matched(0, jnp.where(place < 12, target_a, -1.0))
    hot1, scale1 = matched(1, jnp.where(place >= 12, target_a, -1.0))
    sends[:, :, 0:896] = (
        ((nn(hot0, xs[0]) + nn(hot1, xs[1])) * (scale0 + scale1)).astype(BF16).reshape(16, 16, 896)
    )
    hot, scale = matched(1, target_b)
    rest = jnp.where(place < 8, nn(hot, xs[1, :, 0:512]), nn(hot, xs[1, :, 384:896]))
    sends[:, :, 896:1408] = (rest * scale).astype(BF16).reshape(16, 16, 512)

    def route(i):
        m = (m_me - i + 4) % 4
        if i == 0:
            own = pltpu.make_async_copy(sends.at[z], lands.at[h_me, m_me, p_me], a_recv.at[0])
            own.start()
            others = [(h_me, 1 - p_me), (1 - h_me, 0), (1 - h_me, 1)]
        else:
            others = [(0, 0), (1, 0), (0, 1), (1, 1)]
        for h, p in others:
            zz = h * 8 + m * 2 + p
            remote(
                sends.at[zz], lands.at[h_me, m_me, p_me], a_send, a_recv.at[i], z_dev(zz)
            ).start()

    for i in (0, 1, 3, 2):
        route(i)

    for s in range(2):
        g_buf[x, pl.ds(128 * s, 128), :] = nn(xs[s], select[...]).astype(BF16)

    def g_start():
        for k, sem in ((1, 0), (-1, 1)):
            remote(g_buf.at[x], g_buf.at[x], g_send, g_recv.at[sem], x_dev(k)).start()

    def g_forward():
        left, right = (x + 3) % 4, (x + 1) % 4
        landed(g_buf.at[0], g_recv.at[0])
        part_l = g_buf.at[left, pl.ds(0, 128)]
        remote(part_l, part_l, g_send, g_recv.at[2], x_dev(1)).start()
        landed(g_buf.at[0], g_recv.at[1])
        part_r = g_buf.at[right, pl.ds(128, 128)]
        remote(part_r, part_r, g_send, g_recv.at[3], x_dev(-1)).start()

    def g_wait():
        landed(g_buf.at[0, pl.ds(0, 128)], g_recv.at[2])
        landed(g_buf.at[0, pl.ds(0, 128)], g_recv.at[3])

    def y_index(g, j, plus):
        return 8 * g + 2 * (j - 1) + (0 if plus else 1)

    def y_steps(g, plus):
        return 4 if plus == (g % 2 == 0) else 3

    def y_step(g, j):
        a, b = Z_GROUPS[g]
        for plus in (True, False):
            if j <= y_steps(g, plus):
                origin = (y + (1 - j if plus else j - 1) + 8) % 8
                ref = d_weight.at[origin, pl.ds(a, b - a)]
                remote(ref, ref, y_send, y_recv.at[y_index(g, j, plus)], y_dev(1 if plus else -1)).start()

    def y_wait(g, j):
        a, b = Z_GROUPS[g]
        for plus in (True, False):
            if j <= y_steps(g, plus):
                landed(d_weight.at[0, pl.ds(a, b - a)], y_recv.at[y_index(g, j, plus)])

    qq = iota((96, 128), 0)
    ww = iota((96, 128), 1)
    chip = (
        jnp.where(qq >= 24, 1, 0) + jnp.where(qq >= 48, 1, 0) + jnp.where(qq >= 72, 1, 0)
    )
    row = qq - 24 * chip
    wrow = ww & 15
    same = ((ww >> 4) & 3) == chip
    head = same & (ww < 64) & (row == wrow)
    tail0 = same & (ww >= 64) & (row == wrow + 16) & (wrow < 8)
    tail1 = same & (ww >= 64) & (row == wrow + 8) & (wrow >= 8)
    pick0, pick1 = one_hot(head | tail0), one_hot(head | tail1)

    def group_of(i):
        return (m_me + i) % 4

    def gather_rows(i):
        m = group_of(i)
        landed(lands.at[:, 0], a_recv.at[i])
        got = jnp.concatenate([lands[0, m].reshape(32, 1408), lands[1, m].reshape(32, 1408)], axis=0)
        more = got[:, 896:1408]
        low = nn(pick0, jnp.concatenate([got[:, 0:512], more], axis=0))
        high = nn(pick1, jnp.concatenate([got[:, 512:896], more[:, 128:512]], axis=0))
        full = jnp.concatenate([low, high], axis=1).astype(BF16)
        rows[x, 0, m] = full[0:48]
        rows[x, 1, m] = full[48:96]
        ref = rows.at[x, :, m]
        remote(ref, ref, x_send, x_recv.at[4 * i], x_dev(1)).start()
        remote(ref, ref, x_send, x_recv.at[4 * i + 1], x_dev(-1)).start()

    def forward_rows(i):
        m = group_of(i)
        landed(rows.at[0, :, 0], x_recv.at[4 * i])
        part_l = rows.at[(x + 3) % 4, 0, m]
        remote(part_l, part_l, x_send, x_recv.at[4 * i + 2], x_dev(1)).start()
        landed(rows.at[0, :, 0], x_recv.at[4 * i + 1])
        part_r = rows.at[(x + 1) % 4, 1, m]
        remote(part_r, part_r, x_send, x_recv.at[4 * i + 3], x_dev(-1)).start()

    def end_rows(i):
        landed(rows.at[0, 0, 0], x_recv.at[4 * i + 2])
        landed(rows.at[0, 0, 0], x_recv.at[4 * i + 3])

    def expert_dot(k):
        return nt(weight[k], rows[k].reshape(384, 896))

    g_start()
    z_wait(1)
    z_step(2)
    y_step(0, 1)

    loads[4].wait()
    loads[5].wait()
    fac_gate[...], fac_up[...] = factors(e_gate[...], e_up[...])

    ready = {r: g for g, r in enumerate(Z_READY)}
    g_forward()
    actions = {3: [0], 6: [1], 8: [2]}
    for tick in range(2, 9):
        z_wait(tick)
        if tick < 8:
            z_step(tick + 1)
        if tick in ready:
            y_step(ready[tick], 1)
        for g in range(4):
            j = tick - Z_READY[g]
            if 1 <= j <= 4:
                y_wait(g, j)
                if j < 4:
                    y_step(g, j + 1)
        for i in actions.get(tick, ()):
            gather_rows(i)
            if i:
                forward_rows(i - 1)
    for tick in range(9, 13):
        for g in range(4):
            j = tick - Z_READY[g]
            if 1 <= j <= 4:
                y_wait(g, j)
                if j < 4:
                    y_step(g, j + 1)
        if tick == 9:
            gather_rows(3)
            forward_rows(2)
        if tick == 11:
            forward_rows(3)

    g_wait()
    total = jnp.zeros((256, 640), F32)
    for k in range(4):
        total += nn(g_buf[k], d_weight[2 * k : 2 * k + 2].reshape(512, 640))
    part[...] = total.reshape(2, 128, 640)
    give = remote(part.at[1 - c], part_in, p_send, p_recv, sib)
    give.start()

    for k in range(4):
        loads[8 + k].wait()
    acc[...] = expert_dot(x)

    loads[6].wait()
    loads[7].wait()
    gate_fac, up_fac = factors(d_gate[...], d_up[...])
    give.wait_recv()
    hidden = (part[c] + part_in[...]).T[0:608]
    dgate_out[...] = (hidden * gate_fac).astype(BF16)
    dup_out[...] = (hidden * up_fac).astype(BF16)

    acc[...] += expert_dot((x + 1) % 4)
    acc[...] += expert_dot((x + 3) % 4)
    for i in range(4):
        end_rows(i)
    hidden = acc[...] + expert_dot((x + 2) % 4)
    egate_out[...] = (hidden * fac_gate[...]).astype(BF16)
    eup_out[...] = (hidden * fac_up[...]).astype(BF16)

    for copy in swap:
        copy.wait_send()
    landed(d_weight.at[0, pl.ds(0, 15)], z_send)
    landed(d_weight.at[pl.ds(0, 7)], y_send)
    landed(g_buf.at[pl.ds(0, 3)], g_send)
    landed(rows.at[pl.ds(0, 3)], x_send)
    landed(sends.at[pl.ds(0, 15)], a_send)
    give.wait_send()


def local(
    out_grad, route_ids, route_probs, dense_gate_pre, dense_up_pre, dense_down,
    expert_gate_pre, expert_up_pre, expert_down,
):
    dma = pltpu.SemaphoreType.DMA
    vmem = pltpu.VMEM
    shapes = [
        vmem((2, 128), jnp.int32), vmem((2, 128), F32), vmem((2, 8, 128), F32),
        vmem((2, 128, 896), BF16), vmem((16, 16, 1408), BF16), vmem((2, 4, 2, 16, 1408), BF16),
        vmem((4, 2, 4, 48, 896), BF16), vmem((4, 608, 896), BF16), vmem((608, 384), F32),
        vmem((608, 384), BF16), vmem((608, 384), BF16), vmem((608, 384), F32), vmem((608, 384), F32),
        vmem((14, 608), BF16), vmem((608, 128), BF16), vmem((608, 128), BF16),
        vmem((8, 16, 16, 640), BF16), vmem((4, 256, 512), BF16), vmem((896, 512), BF16),
        vmem((2, 128, 640), F32), vmem((128, 640), F32),
        dma((12,)), dma((2,)), dma((2,)), dma, dma((15,)), dma, dma((32,)), dma, dma((4,)),
        dma, dma((16,)), dma, dma((4,)), dma, dma,
    ]
    any_spec = pl.BlockSpec(memory_space=pl.ANY)
    whole = pl.BlockSpec(memory_space=pltpu.VMEM)
    dgate, dup, egate, eup = pl.pallas_call(
        kernel,
        out_shape=[
            jax.ShapeDtypeStruct((608, 128), BF16), jax.ShapeDtypeStruct((608, 128), BF16),
            jax.ShapeDtypeStruct((608, 384), BF16), jax.ShapeDtypeStruct((608, 384), BF16),
        ],
        in_specs=[any_spec] * 9,
        out_specs=[whole] * 4,
        scratch_shapes=shapes,
        compiler_params=pltpu.CompilerParams(
            collective_id=0, has_side_effects=True, vmem_limit_bytes=48 << 20
        ),
        cost_estimate=pl.CostEstimate(
            flops=2 * 512 * 608 * 3584, bytes_accessed=8 << 20, transcendentals=512 * 608
        ),
    )(
        out_grad, route_ids.T, route_probs.T, dense_gate_pre.T, dense_up_pre.T, dense_down.T,
        expert_gate_pre[0, 0].T, expert_up_pre[0, 0].T, expert_down[0],
    )
    return (
        dgate.T, dup.T, egate.T.reshape(expert_gate_pre.shape), eup.T.reshape(expert_up_pre.shape),
    )


def solution(mesh):
    placed = (
        P(("dp", "expert"), "tensor"),
        P(("dp", "expert"), None),
        P(("dp", "expert"), None),
        P(("dp", "expert"), "tensor"),
        P(("dp", "expert"), "tensor"),
        P("tensor", ("dp", "expert")),
        P("dp", "expert", None, "tensor"),
        P("dp", "expert", None, "tensor"),
        P("expert", "tensor", None),
    )
    return jax.shard_map(
        local,
        mesh=mesh,
        in_specs=placed,
        out_specs=(
            P(("dp", "expert"), "tensor"),
            P(("dp", "expert"), "tensor"),
            P("dp", "expert", None, "tensor"),
            P("dp", "expert", None, "tensor"),
        ),
        check_vma=False,
    )
```

```python
import functools

import jax
import jax.numpy as jnp
from jax import lax
from jax.experimental import pallas as pl
from jax.experimental.pallas import tpu as pltpu
from jax.sharding import PartitionSpec as P

MESH = pl.DeviceIdType.MESH
F32 = jnp.float32
BF16 = jnp.bfloat16

Z_GROUPS = ((0, 3), (3, 7), (7, 11), (11, 16))
Z_READY = (1, 3, 5, 8)
Y_TICKS = {
    4: ((0, 1),), 6: ((0, 2),), 7: ((1, 1),), 8: ((0, 3),), 9: ((1, 2), (2, 1)), 10: ((0, 4),),
    11: ((1, 3), (2, 2), (3, 1)), 12: ((1, 4),), 13: ((2, 3), (3, 2)), 14: ((2, 4), (3, 3)), 15: ((3, 4),),
}


def slot_of(offset):
    if offset == 0:
        return 0
    return 2 * offset - 1 if offset > 0 else -2 * offset


def iota(shape, dim):
    return lax.broadcasted_iota(jnp.int32, shape, dim)


def one_hot(mask):
    return jnp.where(mask, 1.0, 0.0).astype(BF16)


def nn(a, b):
    return jnp.dot(a, b, preferred_element_type=F32)


def nt(a, b):
    return lax.dot_general(a, b, (((1,), (1,)), ((), ())), preferred_element_type=F32)


def factors(gate_pre, up_pre):
    a = gate_pre.astype(F32)
    b = up_pre.astype(F32)
    sigma = 1.0 / (1.0 + jnp.exp(-a))
    return b * sigma * (1.0 + a * (1.0 - sigma)), a * sigma


def kernel(
    grad_in, ids_in, probs_in, dgate_in, dup_in, ddown_in, egate_in, eup_in, edown_in,
    dgate_out, dup_out, egate_out, eup_out,
    ids, probs, table, xs, sends, lands, rows, weight, acc, e_gate, e_up, fac_gate, fac_up,
    d_raw, d_gate, d_up, d_weight, g_buf, select, part, part_in,
    in_sem, sib_send, sib_recv, z_send, z_recv, y_send, y_recv, g_send, g_recv,
    x_send, x_recv, a_send, a_recv, p_send, p_recv,
):
    y = lax.axis_index("dp")
    e = lax.axis_index("expert")
    x = lax.axis_index("tensor")
    z, c = e // 2, e % 2
    sib = (y, e + 1 - 2 * c, x)
    z_dev = lambda zz: (y, 2 * zz + c, x)
    y_dev = lambda k: ((y + k + 8) % 8, e, x)
    x_dev = lambda k: (y, e, (x + k + 4) % 4)
    pair, half = z // 2, z % 2

    def remote(src, dst, send, recv, dev):
        return pltpu.make_async_remote_copy(
            src_ref=src, dst_ref=dst, send_sem=send, recv_sem=recv, device_id=dev, device_id_type=MESH
        )

    def landed(ref, sem):
        pltpu.make_async_copy(ref, ref, sem).wait()

    barrier = pltpu.get_barrier_semaphore()

    def greet(k, carry):
        pl.semaphore_signal(barrier, inc=1, device_id=z_dev((z + k) % 16), device_id_type=MESH)
        return carry

    for dev in (sib, y_dev(1), y_dev(-1), x_dev(1), x_dev(-1)):
        pl.semaphore_signal(barrier, inc=1, device_id=dev, device_id_type=MESH)
    lax.fori_loop(1, 16, greet, 0)

    loads = [
        (ids_in, ids), (probs_in, probs), (grad_in, xs.at[c]), (ddown_in, d_raw),
        (egate_in, e_gate), (eup_in, e_up), (dgate_in, d_gate), (dup_in, d_up),
    ] + [(edown_in.at[:, pl.ds(896 * k, 896)], weight.at[k]) for k in range(4)]
    loads = [pltpu.make_async_copy(s, d, in_sem.at[i]) for i, (s, d) in enumerate(loads)]
    for copy in loads:
        copy.start()

    loads[3].wait()
    d_weight[y, 0] = jnp.concatenate(
        [
            jnp.concatenate([d_raw[...].astype(F32), jnp.zeros((14, 32), F32)], axis=1),
            jnp.zeros((2, 640), F32),
        ],
        axis=0,
    ).astype(BF16)

    loads[0].wait()
    loads[1].wait()
    experts = iota((32, 128), 0)
    first, second = experts == ids[0:1, :], experts == ids[1:2, :]
    named = one_hot(first) + one_hot(second)
    earlier = nn(named, one_hot(iota((128, 128), 0) < iota((128, 128), 1)))
    cell_of = lambda j, hot: ids[j : j + 1, :].astype(F32) * 12.0 + jnp.sum(
        jnp.where(hot, earlier, 0.0), axis=0, keepdims=True
    )
    table[c] = jnp.concatenate(
        [cell_of(0, first), cell_of(1, second), probs[...], jnp.zeros((4, 128), F32)], axis=0
    )
    loads[2].wait()

    pl.semaphore_wait(barrier, 20)

    swap = [
        remote(table.at[c], table.at[c], sib_send.at[0], sib_recv.at[0], sib),
        remote(xs.at[c], xs.at[c], sib_send.at[1], sib_recv.at[1], sib),
    ]
    for copy in swap:
        copy.start()

    def z_step(s):
        plus = remote(
            d_weight.at[y, slot_of(1 - s)], d_weight.at[y, 15 if s == 8 else slot_of(-s)],
            z_send, z_recv.at[2 * s - 2], z_dev((z + 1) % 16),
        )
        plus.start()
        if s < 8:
            remote(
                d_weight.at[y, slot_of(s - 1)], d_weight.at[y, slot_of(s)],
                z_send, z_recv.at[2 * s - 1], z_dev((z + 15) % 16),
            ).start()

    def z_wait(s):
        landed(d_weight.at[y, 0], z_recv.at[2 * s - 2])
        if s < 8:
            landed(d_weight.at[y, 0], z_recv.at[2 * s - 1])

    z_step(1)

    q = iota((1, 512), 1)
    slot = (q >> 4) & 15
    half_off = (slot + 1) >> 1
    zq = (z + jnp.where((slot & 1) == 1, half_off, 16 - half_off)) & 15
    target = jnp.where((q & 15) < 14, (((q >> 8) * 16 + zq) * 2 + c) * 14 + (q & 15), -1)
    for k in range(7):
        select[pl.ds(128 * k, 128), :] = one_hot(iota((128, 512), 0) + 128 * k == target)

    z_wait(1)
    z_step(2)
    for copy in swap:
        copy.wait_recv()

    w = iota((256, 1), 0)
    place = w & 15
    base = (2 * (w >> 4) + c) * 12
    target_a = jnp.where(place < 12, base + place, base + place - 12).astype(F32)
    target_b = (base + 4 + (place & 7)).astype(F32)

    def matched(core, wanted):
        tab = table[core]
        hit0, hit1 = tab[0:1, :] == wanted, tab[1:2, :] == wanted
        scale = jnp.sum(
            jnp.where(hit0, tab[2:3, :], 0.0) + jnp.where(hit1, tab[3:4, :], 0.0), axis=1, keepdims=True
        )
        return one_hot(hit0 | hit1), scale

    hot0, scale0 = matched(0, jnp.where(place < 12, target_a, -1.0))
    hot1, scale1 = matched(1, jnp.where(place >= 12, target_a, -1.0))
    sends[:, :, 0:896] = (
        ((nn(hot0, xs[0]) + nn(hot1, xs[1])) * (scale0 + scale1)).astype(BF16).reshape(16, 16, 896)
    )
    z_wait(2)
    z_step(3)
    hot, scale = matched(1, target_b)
    rest = jnp.where(place < 8, nn(hot, xs[1, :, 0:512]), nn(hot, xs[1, :, 384:896]))
    sends[:, :, 896:1408] = (rest * scale).astype(BF16).reshape(16, 16, 512)

    def group_of(i):
        return (pair + i) % 8, (pair + (4 if i == 0 else 8 - i)) % 8

    def route(i):
        near, far = group_of(i)
        spots = [(near, 0), (near, 1), (far, 0), (far, 1)]
        if i == 0:
            pltpu.make_async_copy(sends.at[z], lands.at[pair, half], a_recv.at[0]).start()
            spots = [(near, 1 - half)] + spots[2:]
        for m, p in spots:
            zz = m * 2 + p
            remote(sends.at[zz], lands.at[pair, half], a_send, a_recv.at[i], z_dev(zz)).start()

    def g_start():
        for k, sem in ((1, 0), (-1, 1)):
            remote(g_buf.at[x], g_buf.at[x], g_send, g_recv.at[sem], x_dev(k)).start()

    def g_forward():
        left, right = (x + 3) % 4, (x + 1) % 4
        landed(g_buf.at[0], g_recv.at[0])
        part_l = g_buf.at[left, pl.ds(0, 128)]
        remote(part_l, part_l, g_send, g_recv.at[2], x_dev(1)).start()
        landed(g_buf.at[0], g_recv.at[1])
        part_r = g_buf.at[right, pl.ds(128, 128)]
        remote(part_r, part_r, g_send, g_recv.at[3], x_dev(-1)).start()

    def g_wait():
        landed(g_buf.at[0, pl.ds(0, 128)], g_recv.at[2])
        landed(g_buf.at[0, pl.ds(0, 128)], g_recv.at[3])

    def y_index(g, j, plus):
        return 8 * g + 2 * (j - 1) + (0 if plus else 1)

    def y_span(g, j, plus):
        a, b = Z_GROUPS[g]
        mid = (a + b + g % 2) // 2
        return (a, b) if j < 4 else ((a, mid) if plus else (mid, b))

    def y_step(g, j):
        for plus in (True, False):
            a, b = y_span(g, j, plus)
            origin = (y + (1 - j if plus else j - 1) + 8) % 8
            ref = d_weight.at[origin, pl.ds(a, b - a)]
            remote(ref, ref, y_send, y_recv.at[y_index(g, j, plus)], y_dev(1 if plus else -1)).start()

    def y_wait(g, j):
        for plus in (True, False):
            a, b = y_span(g, j, plus)
            landed(d_weight.at[0, pl.ds(a, b - a)], y_recv.at[y_index(g, j, plus)])

    qq = iota((96, 128), 0)
    ww = iota((96, 128), 1)
    chip = (
        jnp.where(qq >= 24, 1, 0) + jnp.where(qq >= 48, 1, 0) + jnp.where(qq >= 72, 1, 0)
    )
    row = qq - 24 * chip
    wrow = ww & 15
    same = ((ww >> 4) & 3) == chip
    head = same & (ww < 64) & (row == wrow)
    tail0 = same & (ww >= 64) & (row == wrow + 16) & (wrow < 8)
    tail1 = same & (ww >= 64) & (row == wrow + 8) & (wrow >= 8)
    pick0, pick1 = one_hot(head | tail0), one_hot(head | tail1)

    def gather_rows(i):
        blocks = group_of(i)
        landed(lands.at[pl.ds(0, 2)], a_recv.at[i])
        got = jnp.concatenate([lands[m].reshape(32, 1408) for m in blocks], axis=0)
        more = got[:, 896:1408]
        low = nn(pick0, jnp.concatenate([got[:, 0:512], more], axis=0))
        high = nn(pick1, jnp.concatenate([got[:, 512:896], more[:, 128:512]], axis=0))
        full = jnp.concatenate([low, high], axis=1).astype(BF16)
        for k, m in enumerate(blocks):
            rows[x, m] = full[48 * k : 48 * k + 48]
        for m in blocks:
            ref = rows.at[x, m]
            remote(ref, ref, x_send, x_recv.at[4 * i], x_dev(1)).start()
            remote(ref, ref, x_send, x_recv.at[4 * i + 1], x_dev(-1)).start()

    def forward_rows(i):
        near, far = group_of(i)
        landed(rows.at[0, pl.ds(0, 2)], x_recv.at[4 * i])
        part_l = rows.at[(x + 3) % 4, near]
        remote(part_l, part_l, x_send, x_recv.at[4 * i + 2], x_dev(1)).start()
        landed(rows.at[0, pl.ds(0, 2)], x_recv.at[4 * i + 1])
        part_r = rows.at[(x + 1) % 4, far]
        remote(part_r, part_r, x_send, x_recv.at[4 * i + 3], x_dev(-1)).start()

    def end_rows(i):
        landed(rows.at[0, 0], x_recv.at[4 * i + 2])
        landed(rows.at[0, 0], x_recv.at[4 * i + 3])

    def expert_dot(k):
        return nt(weight[k], rows[k].reshape(384, 896))

    def tick(t):
        if t <= 8:
            z_wait(t)
            if t < 8:
                z_step(t + 1)
            if t in Z_READY:
                y_step(Z_READY.index(t), 1)
        for g, j in Y_TICKS.get(t, ()):
            y_wait(g, j)
            if j < 4:
                y_step(g, j + 1)

    y_step(0, 1)
    route(3)
    for t in (3, 4):
        tick(t)
    route(2)
    for s in range(2):
        g_buf[x, pl.ds(128 * s, 128), :] = nn(xs[s], select[...]).astype(BF16)
    g_start()
    for t in (5, 6, 7, 8):
        tick(t)
    route(0)

    loads[4].wait()
    loads[5].wait()
    fac_gate[...], fac_up[...] = factors(e_gate[...], e_up[...])
    g_forward()
    for t in (9,):
        tick(t)
    gather_rows(3)
    route(1)
    for t in (10, 11,):
        tick(t)
    forward_rows(3)
    gather_rows(2)
    for t in (12,):
        tick(t)
    for t in (13, 14):
        tick(t)
    forward_rows(2)
    gather_rows(0)
    for t in (15,):
        tick(t)

    g_wait()
    total = jnp.zeros((256, 640), F32)
    for k in range(4):
        total += nn(g_buf[k], d_weight[2 * k : 2 * k + 2].reshape(512, 640))
    part[...] = total.reshape(2, 128, 640)
    give = remote(part.at[1 - c], part_in, p_send, p_recv, sib)
    give.start()
    gather_rows(1)
    forward_rows(0)

    for k in range(4):
        loads[8 + k].wait()
    acc[...] = expert_dot(x)

    forward_rows(1)
    loads[6].wait()
    loads[7].wait()
    gate_fac, up_fac = factors(d_gate[...], d_up[...])
    give.wait_recv()
    hidden = (part[c] + part_in[...]).T[0:608]
    dgate_out[...] = (hidden * gate_fac).astype(BF16)
    dup_out[...] = (hidden * up_fac).astype(BF16)

    acc[...] += expert_dot((x + 1) % 4) + expert_dot((x + 3) % 4)
    for i in range(4):
        end_rows(i)
    hidden = acc[...] + expert_dot((x + 2) % 4)
    egate_out[...] = (hidden * fac_gate[...]).astype(BF16)
    eup_out[...] = (hidden * fac_up[...]).astype(BF16)

    for copy in swap:
        copy.wait_send()
    landed(d_weight.at[0, pl.ds(0, 15)], z_send)
    landed(d_weight.at[pl.ds(0, 7)], y_send)
    landed(g_buf.at[pl.ds(0, 3)], g_send)
    landed(rows.at[pl.ds(0, 3)], x_send)
    landed(sends.at[pl.ds(0, 15)], a_send)
    give.wait_send()


def local(
    out_grad, route_ids, route_probs, dense_gate_pre, dense_up_pre, dense_down,
    expert_gate_pre, expert_up_pre, expert_down,
):
    dma = pltpu.SemaphoreType.DMA
    vmem = pltpu.VMEM
    shapes = [
        vmem((2, 128), jnp.int32), vmem((2, 128), F32), vmem((2, 8, 128), F32),
        vmem((2, 128, 896), BF16), vmem((16, 16, 1408), BF16), vmem((8, 2, 16, 1408), BF16),
        vmem((4, 8, 48, 896), BF16), vmem((4, 608, 896), BF16), vmem((608, 384), F32),
        vmem((608, 384), BF16), vmem((608, 384), BF16), vmem((608, 384), F32), vmem((608, 384), F32),
        vmem((14, 608), BF16), vmem((608, 128), BF16), vmem((608, 128), BF16),
        vmem((8, 16, 16, 640), BF16), vmem((4, 256, 512), BF16), vmem((896, 512), BF16),
        vmem((2, 128, 640), F32), vmem((128, 640), F32),
        dma((12,)), dma((2,)), dma((2,)), dma, dma((15,)), dma, dma((32,)), dma, dma((4,)),
        dma, dma((16,)), dma, dma((4,)), dma, dma,
    ]
    any_spec = pl.BlockSpec(memory_space=pltpu.HBM)
    whole = pl.BlockSpec(memory_space=pltpu.VMEM)
    dgate, dup, egate, eup = pl.pallas_call(
        kernel,
        out_shape=[
            jax.ShapeDtypeStruct((608, 128), BF16), jax.ShapeDtypeStruct((608, 128), BF16),
            jax.ShapeDtypeStruct((608, 384), BF16), jax.ShapeDtypeStruct((608, 384), BF16),
        ],
        in_specs=[any_spec] * 9,
        out_specs=[whole] * 4,
        scratch_shapes=shapes,
        compiler_params=pltpu.CompilerParams(
            collective_id=0, has_side_effects=True, vmem_limit_bytes=62 << 20
        ),
        cost_estimate=pl.CostEstimate(
            flops=2 * 512 * 608 * 3584, bytes_accessed=8 << 20, transcendentals=512 * 608
        ),
    )(
        out_grad, route_ids.T, route_probs.T, dense_gate_pre.T, dense_up_pre.T, dense_down.T,
        expert_gate_pre[0, 0].T, expert_up_pre[0, 0].T, expert_down[0],
    )
    return (
        dgate.T, dup.T, egate.T.reshape(expert_gate_pre.shape), eup.T.reshape(expert_up_pre.shape),
    )


def solution(mesh):
    placed = (
        P(("dp", "expert"), "tensor"),
        P(("dp", "expert"), None),
        P(("dp", "expert"), None),
        P(("dp", "expert"), "tensor"),
        P(("dp", "expert"), "tensor"),
        P("tensor", ("dp", "expert")),
        P("dp", "expert", None, "tensor"),
        P("dp", "expert", None, "tensor"),
        P("expert", "tensor", None),
    )
    return jax.shard_map(
        local,
        mesh=mesh,
        in_specs=placed,
        out_specs=(
            P(("dp", "expert"), "tensor"),
            P(("dp", "expert"), "tensor"),
            P("dp", "expert", None, "tensor"),
            P("dp", "expert", None, "tensor"),
        ),
        check_vma=False,
    )
```

```python
import functools

import jax
import jax.numpy as jnp
from jax import lax
from jax.experimental import pallas as pl
from jax.experimental.pallas import tpu as pltpu
from jax.sharding import PartitionSpec as P

MESH = pl.DeviceIdType.MESH
F32 = jnp.float32
BF16 = jnp.bfloat16

Z_GROUPS = ((0, 3), (3, 7), (7, 11), (11, 16))
Z_READY = (1, 3, 5, 8)
Y_TICKS = {
    4: ((0, 1),), 6: ((0, 2),), 7: ((1, 1),), 8: ((0, 3),), 9: ((1, 2), (2, 1)), 10: ((0, 4),),
    11: ((1, 3), (2, 2), (3, 1)), 12: ((1, 4),), 13: ((2, 3), (3, 2)), 14: ((2, 4), (3, 3)), 15: ((3, 4),),
}


def slot_of(offset):
    if offset == 0:
        return 0
    return 2 * offset - 1 if offset > 0 else -2 * offset


def iota(shape, dim):
    return lax.broadcasted_iota(jnp.int32, shape, dim)


def one_hot(mask):
    return jnp.where(mask, 1.0, 0.0).astype(BF16)


def nn(a, b):
    return jnp.dot(a, b, preferred_element_type=F32)


def nt(a, b):
    return lax.dot_general(a, b, (((1,), (1,)), ((), ())), preferred_element_type=F32)


def factors(gate_pre, up_pre):
    a = gate_pre.astype(F32)
    b = up_pre.astype(F32)
    sigma = 1.0 / (1.0 + jnp.exp(-a))
    return b * sigma * (1.0 + a * (1.0 - sigma)), a * sigma


def kernel(
    grad_in, ids_in, probs_in, dgate_in, dup_in, ddown_in, egate_in, eup_in, edown_in,
    dgate_out, dup_out, egate_out, eup_out,
    ids, probs, table, xs, sends, lands, rows, weight, acc, e_gate, e_up, fac_gate, fac_up,
    d_raw, d_gate, d_up, d_weight, g_buf, select, part, part_in,
    in_sem, sib_send, sib_recv, z_send, z_recv, y_send, y_recv, g_send, g_recv,
    x_send, x_recv, a_send, a_recv, p_send, p_recv,
):
    y = lax.axis_index("dp")
    e = lax.axis_index("expert")
    x = lax.axis_index("tensor")
    z, c = e // 2, e % 2
    sib = (y, e + 1 - 2 * c, x)
    z_dev = lambda zz: (y, 2 * zz + c, x)
    y_dev = lambda k: ((y + k + 8) % 8, e, x)
    x_dev = lambda k: (y, e, (x + k + 4) % 4)
    pair, half = z // 2, z % 2

    def remote(src, dst, send, recv, dev):
        return pltpu.make_async_remote_copy(
            src_ref=src, dst_ref=dst, send_sem=send, recv_sem=recv, device_id=dev, device_id_type=MESH
        )

    def landed(ref, sem):
        pltpu.make_async_copy(ref, ref, sem).wait()

    barrier = pltpu.get_barrier_semaphore()

    def greet(k, carry):
        pl.semaphore_signal(barrier, inc=1, device_id=z_dev((z + k) % 16), device_id_type=MESH)
        return carry

    for dev in (sib, y_dev(1), y_dev(-1), x_dev(1), x_dev(-1)):
        pl.semaphore_signal(barrier, inc=1, device_id=dev, device_id_type=MESH)
    lax.fori_loop(1, 16, greet, 0)

    loads = [
        (ids_in, ids), (probs_in, probs), (grad_in, xs.at[c]), (ddown_in, d_raw),
        (egate_in, e_gate), (eup_in, e_up), (dgate_in, d_gate), (dup_in, d_up),
    ] + [(edown_in.at[:, pl.ds(896 * k, 896)], weight.at[k]) for k in range(4)]
    loads = [pltpu.make_async_copy(s, d, in_sem.at[i]) for i, (s, d) in enumerate(loads)]
    for copy in loads:
        copy.start()

    loads[3].wait()
    d_weight[y, 0] = jnp.concatenate(
        [
            jnp.concatenate([d_raw[...].astype(F32), jnp.zeros((14, 32), F32)], axis=1),
            jnp.zeros((2, 640), F32),
        ],
        axis=0,
    ).astype(BF16)

    loads[0].wait()
    loads[1].wait()
    experts = iota((32, 128), 0)
    first, second = experts == ids[0:1, :], experts == ids[1:2, :]
    named = one_hot(first) + one_hot(second)
    earlier = nn(named, one_hot(iota((128, 128), 0) < iota((128, 128), 1)))
    cell_of = lambda j, hot: ids[j : j + 1, :].astype(F32) * 12.0 + jnp.sum(
        jnp.where(hot, earlier, 0.0), axis=0, keepdims=True
    )
    table[c] = jnp.concatenate(
        [cell_of(0, first), cell_of(1, second), probs[...], jnp.zeros((4, 128), F32)], axis=0
    )
    loads[2].wait()

    pl.semaphore_wait(barrier, 20)

    swap = [
        remote(table.at[c], table.at[c], sib_send.at[0], sib_recv.at[0], sib),
        remote(xs.at[c], xs.at[c], sib_send.at[1], sib_recv.at[1], sib),
    ]
    for copy in swap:
        copy.start()

    def z_step(s):
        plus = remote(
            d_weight.at[y, slot_of(1 - s)], d_weight.at[y, 15 if s == 8 else slot_of(-s)],
            z_send, z_recv.at[2 * s - 2], z_dev((z + 1) % 16),
        )
        plus.start()
        if s < 8:
            remote(
                d_weight.at[y, slot_of(s - 1)], d_weight.at[y, slot_of(s)],
                z_send, z_recv.at[2 * s - 1], z_dev((z + 15) % 16),
            ).start()

    def z_wait(s):
        landed(d_weight.at[y, 0], z_recv.at[2 * s - 2])
        if s < 8:
            landed(d_weight.at[y, 0], z_recv.at[2 * s - 1])

    z_step(1)

    q = iota((1, 512), 1)
    slot = (q >> 4) & 15
    half_off = (slot + 1) >> 1
    zq = (z + jnp.where((slot & 1) == 1, half_off, 16 - half_off)) & 15
    target = jnp.where((q & 15) < 14, (((q >> 8) * 16 + zq) * 2 + c) * 14 + (q & 15), -1)
    for k in range(7):
        select[pl.ds(128 * k, 128), :] = one_hot(iota((128, 512), 0) + 128 * k == target)

    z_wait(1)
    z_step(2)
    for copy in swap:
        copy.wait_recv()

    w = iota((256, 1), 0)
    place = w & 15
    base = (2 * (w >> 4) + c) * 12
    target_a = jnp.where(place < 12, base + place, base + place - 12).astype(F32)
    target_b = (base + 4 + (place & 7)).astype(F32)

    def matched(core, wanted):
        tab = table[core]
        hit0, hit1 = tab[0:1, :] == wanted, tab[1:2, :] == wanted
        scale = jnp.sum(
            jnp.where(hit0, tab[2:3, :], 0.0) + jnp.where(hit1, tab[3:4, :], 0.0), axis=1, keepdims=True
        )
        return one_hot(hit0 | hit1), scale

    hot0, scale0 = matched(0, jnp.where(place < 12, target_a, -1.0))
    hot1, scale1 = matched(1, jnp.where(place >= 12, target_a, -1.0))
    sends[:, :, 0:896] = (
        ((nn(hot0, xs[0]) + nn(hot1, xs[1])) * (scale0 + scale1)).astype(BF16).reshape(16, 16, 896)
    )
    z_wait(2)
    z_step(3)
    hot, scale = matched(1, target_b)
    rest = jnp.where(place < 8, nn(hot, xs[1, :, 0:512]), nn(hot, xs[1, :, 384:896]))
    sends[:, :, 896:1408] = (rest * scale).astype(BF16).reshape(16, 16, 512)

    def group_of(i):
        return (pair + i) % 8, (pair + (4 if i == 0 else 8 - i)) % 8

    def route(i):
        near, far = group_of(i)
        spots = [(near, 0), (near, 1), (far, 0), (far, 1)]
        if i == 0:
            pltpu.make_async_copy(sends.at[z], lands.at[pair, half], a_recv.at[0]).start()
            spots = [(near, 1 - half)] + spots[2:]
        for m, p in spots:
            zz = m * 2 + p
            remote(sends.at[zz], lands.at[pair, half], a_send, a_recv.at[i], z_dev(zz)).start()

    def g_start():
        for k, sem in ((1, 0), (-1, 1)):
            remote(g_buf.at[x], g_buf.at[x], g_send, g_recv.at[sem], x_dev(k)).start()

    def g_forward():
        left, right = (x + 3) % 4, (x + 1) % 4
        landed(g_buf.at[0], g_recv.at[0])
        part_l = g_buf.at[left, pl.ds(0, 128)]
        remote(part_l, part_l, g_send, g_recv.at[2], x_dev(1)).start()
        landed(g_buf.at[0], g_recv.at[1])
        part_r = g_buf.at[right, pl.ds(128, 128)]
        remote(part_r, part_r, g_send, g_recv.at[3], x_dev(-1)).start()

    def g_wait():
        landed(g_buf.at[0, pl.ds(0, 128)], g_recv.at[2])
        landed(g_buf.at[0, pl.ds(0, 128)], g_recv.at[3])

    def y_index(g, j, plus):
        return 8 * g + 2 * (j - 1) + (0 if plus else 1)

    def y_span(g, j, plus):
        a, b = Z_GROUPS[g]
        mid = (a + b + g % 2) // 2
        return (a, b) if j < 4 else ((a, mid) if plus else (mid, b))

    def y_step(g, j):
        for plus in (True, False):
            a, b = y_span(g, j, plus)
            origin = (y + (1 - j if plus else j - 1) + 8) % 8
            ref = d_weight.at[origin, pl.ds(a, b - a)]
            remote(ref, ref, y_send, y_recv.at[y_index(g, j, plus)], y_dev(1 if plus else -1)).start()

    def y_wait(g, j):
        for plus in (True, False):
            a, b = y_span(g, j, plus)
            landed(d_weight.at[0, pl.ds(a, b - a)], y_recv.at[y_index(g, j, plus)])

    qq = iota((96, 128), 0)
    ww = iota((96, 128), 1)
    chip = (
        jnp.where(qq >= 24, 1, 0) + jnp.where(qq >= 48, 1, 0) + jnp.where(qq >= 72, 1, 0)
    )
    row = qq - 24 * chip
    wrow = ww & 15
    same = ((ww >> 4) & 3) == chip
    head = same & (ww < 64) & (row == wrow)
    tail0 = same & (ww >= 64) & (row == wrow + 16) & (wrow < 8)
    tail1 = same & (ww >= 64) & (row == wrow + 8) & (wrow >= 8)
    pick0, pick1 = one_hot(head | tail0), one_hot(head | tail1)

    def gather_rows(i):
        blocks = group_of(i)
        landed(lands.at[pl.ds(0, 2)], a_recv.at[i])
        got = jnp.concatenate([lands[m].reshape(32, 1408) for m in blocks], axis=0)
        more = got[:, 896:1408]
        low = nn(pick0, jnp.concatenate([got[:, 0:512], more], axis=0))
        high = nn(pick1, jnp.concatenate([got[:, 512:896], more[:, 128:512]], axis=0))
        full = jnp.concatenate([low, high], axis=1).astype(BF16)
        for k, m in enumerate(blocks):
            rows[x, m] = full[48 * k : 48 * k + 48]
        for m in blocks:
            ref = rows.at[x, m]
            remote(ref, ref, x_send, x_recv.at[4 * i], x_dev(1)).start()
            remote(ref, ref, x_send, x_recv.at[4 * i + 1], x_dev(-1)).start()

    def forward_rows(i):
        near, far = group_of(i)
        landed(rows.at[0, pl.ds(0, 2)], x_recv.at[4 * i])
        part_l = rows.at[(x + 3) % 4, near]
        remote(part_l, part_l, x_send, x_recv.at[4 * i + 2], x_dev(1)).start()
        landed(rows.at[0, pl.ds(0, 2)], x_recv.at[4 * i + 1])
        part_r = rows.at[(x + 1) % 4, far]
        remote(part_r, part_r, x_send, x_recv.at[4 * i + 3], x_dev(-1)).start()

    def end_rows(i):
        landed(rows.at[0, 0], x_recv.at[4 * i + 2])
        landed(rows.at[0, 0], x_recv.at[4 * i + 3])

    def expert_dot(k):
        return nt(weight[k], rows[k].reshape(384, 896))

    def tick(t):
        if t <= 8:
            z_wait(t)
            if t < 8:
                z_step(t + 1)
            if t in Z_READY:
                y_step(Z_READY.index(t), 1)
        for g, j in Y_TICKS.get(t, ()):
            y_wait(g, j)
            if j < 4:
                y_step(g, j + 1)

    y_step(0, 1)
    route(1)
    for t in (3, 4):
        tick(t)
    route(0)
    for s in range(2):
        g_buf[x, pl.ds(128 * s, 128), :] = nn(xs[s], select[...]).astype(BF16)
    g_start()
    for t in (5, 6, 7, 8):
        tick(t)
    route(2)

    loads[4].wait()
    loads[5].wait()
    fac_gate[...], fac_up[...] = factors(e_gate[...], e_up[...])
    g_forward()
    tick(9)
    gather_rows(1)
    route(3)
    tick(10)
    tick(11)
    forward_rows(1)
    gather_rows(0)
    tick(12)
    forward_rows(0)
    gather_rows(2)
    tick(13)
    gather_rows(3)
    forward_rows(2)
    tick(14)
    forward_rows(3)
    tick(15)

    g_wait()
    total = jnp.zeros((256, 640), F32)
    for k in range(4):
        total += nn(g_buf[k], d_weight[2 * k : 2 * k + 2].reshape(512, 640))
    part[...] = total.reshape(2, 128, 640)
    give = remote(part.at[1 - c], part_in, p_send, p_recv, sib)
    give.start()
    for k in range(4):
        loads[8 + k].wait()
    acc[...] = expert_dot(x)
    acc[...] += expert_dot((x + 1) % 4) + expert_dot((x + 3) % 4)
    loads[6].wait()
    loads[7].wait()
    gate_fac, up_fac = factors(d_gate[...], d_up[...])
    give.wait_recv()
    hidden = (part[c] + part_in[...]).T[0:608]
    dgate_out[...] = (hidden * gate_fac).astype(BF16)
    dup_out[...] = (hidden * up_fac).astype(BF16)

    for i in range(4):
        end_rows(i)
    hidden = acc[...] + expert_dot((x + 2) % 4)
    egate_out[...] = (hidden * fac_gate[...]).astype(BF16)
    eup_out[...] = (hidden * fac_up[...]).astype(BF16)

    for copy in swap:
        copy.wait_send()
    landed(d_weight.at[0, pl.ds(0, 15)], z_send)
    landed(d_weight.at[pl.ds(0, 7)], y_send)
    landed(g_buf.at[pl.ds(0, 3)], g_send)
    landed(rows.at[pl.ds(0, 3)], x_send)
    landed(sends.at[pl.ds(0, 15)], a_send)
    give.wait_send()


def local(
    out_grad, route_ids, route_probs, dense_gate_pre, dense_up_pre, dense_down,
    expert_gate_pre, expert_up_pre, expert_down,
):
    dma = pltpu.SemaphoreType.DMA
    vmem = pltpu.VMEM
    shapes = [
        vmem((2, 128), jnp.int32), vmem((2, 128), F32), vmem((2, 8, 128), F32),
        vmem((2, 128, 896), BF16), vmem((16, 16, 1408), BF16), vmem((8, 2, 16, 1408), BF16),
        vmem((4, 8, 48, 896), BF16), vmem((4, 608, 896), BF16), vmem((608, 384), F32),
        vmem((608, 384), BF16), vmem((608, 384), BF16), vmem((608, 384), F32), vmem((608, 384), F32),
        vmem((14, 608), BF16), vmem((608, 128), BF16), vmem((608, 128), BF16),
        vmem((8, 16, 16, 640), BF16), vmem((4, 256, 512), BF16), vmem((896, 512), BF16),
        vmem((2, 128, 640), F32), vmem((128, 640), F32),
        dma((12,)), dma((2,)), dma((2,)), dma, dma((15,)), dma, dma((32,)), dma, dma((4,)),
        dma, dma((16,)), dma, dma((4,)), dma, dma,
    ]
    any_spec = pl.BlockSpec(memory_space=pltpu.HBM)
    whole = pl.BlockSpec(memory_space=pltpu.VMEM)
    dgate, dup, egate, eup = pl.pallas_call(
        kernel,
        out_shape=[
            jax.ShapeDtypeStruct((608, 128), BF16), jax.ShapeDtypeStruct((608, 128), BF16),
            jax.ShapeDtypeStruct((608, 384), BF16), jax.ShapeDtypeStruct((608, 384), BF16),
        ],
        in_specs=[any_spec] * 9,
        out_specs=[whole] * 4,
        scratch_shapes=shapes,
        compiler_params=pltpu.CompilerParams(
            collective_id=0, has_side_effects=True, vmem_limit_bytes=62 << 20
        ),
        cost_estimate=pl.CostEstimate(
            flops=2 * 512 * 608 * 3584, bytes_accessed=8 << 20, transcendentals=512 * 608
        ),
    )(
        out_grad, route_ids.T, route_probs.T, dense_gate_pre.T, dense_up_pre.T, dense_down.T,
        expert_gate_pre[0, 0].T, expert_up_pre[0, 0].T, expert_down[0],
    )
    return (
        dgate.T, dup.T, egate.T.reshape(expert_gate_pre.shape), eup.T.reshape(expert_up_pre.shape),
    )


def solution(mesh):
    placed = (
        P(("dp", "expert"), "tensor"),
        P(("dp", "expert"), None),
        P(("dp", "expert"), None),
        P(("dp", "expert"), "tensor"),
        P(("dp", "expert"), "tensor"),
        P("tensor", ("dp", "expert")),
        P("dp", "expert", None, "tensor"),
        P("dp", "expert", None, "tensor"),
        P("expert", "tensor", None),
    )
    return jax.shard_map(
        local,
        mesh=mesh,
        in_specs=placed,
        out_specs=(
            P(("dp", "expert"), "tensor"),
            P(("dp", "expert"), "tensor"),
            P("dp", "expert", None, "tensor"),
            P("dp", "expert", None, "tensor"),
        ),
        check_vma=False,
    )
```
